256 devices in a mesh: box: 32 (over z, y), face: 8 (over x, core).
Axes of the slice: x: 4, y: 4, z: 8, core: 2. Of those that a mesh axis runs over, the one named last changes fastest.
Arguments:
- blocks: bfloat16 [128, 24, 24, 128, 128], P('box', 'face'), may hold values from -1 to 2
- pattern: int32 [128, 24, 24], P('box', 'face'), may hold values from 0 to 1, as said below
- shared: int32 [128, 4], P('box'), may hold values from 0 to 23, as said below
- sketch: bfloat16 [3072, 256], replicated, may hold values from -6 to 6
Outputs:
- merged: bfloat16 [128, 3072, 256], P('box', 'face')
The draws below stay inside these ranges and needn't reach their ends.
Inputs may be any that keep to these rules, and one draw needn't show every extreme that they name: `pattern`: 1 where a block is stored; every diagonal block is stored. `shared`: 4 distinct block indices in increasing order.
All inputs are finite; a program needn't handle non-finite values.
Results may differ from the reference program's by a relative error of at most 0.0085.
Values may be sent and summed in bfloat16 or wider, within the bound.
A program may use at most 128 MiB of HBM per device.

```python
import math
import jax
import jax.numpy as jnp
from jax import lax

BLK = 128
NB = 24
NI = 4
COLS = 256
ITERS = 4
BOX_DEV = 4
BOXES = 128
ORDER = 3072
N_BOX = 32


def draw_blocks(key, part):
    shape = (BOXES, NB, NB, BLK, BLK)
    sigma = 0.8 / math.sqrt(NI * BLK)
    key_noise = jax.random.fold_in(key, 11)
    key_diag = jax.random.fold_in(key, 12)
    noise = jnp.clip(jax.random.normal(key_noise, shape, jnp.float32), -6.0, 6.0) * sigma
    diag_vals = jnp.exp(jax.random.uniform(key_diag, shape, jnp.float32, math.log(0.6), math.log(1.2)))
    row_block = lax_iota_like(NB, 1)
    col_block = lax_iota_like(NB, 2)
    row_cell = lax_iota_like(BLK, 3)
    col_cell = lax_iota_like(BLK, 4)
    on_diag = jnp.logical_and(row_block == col_block, row_cell == col_cell).astype(jnp.float32)
    return (noise + on_diag * diag_vals).astype(jnp.bfloat16)


def lax_iota_like(length, axis_pos):
    dims = [1, 1, 1, 1, 1]
    dims[axis_pos] = length
    return jnp.arange(length, dtype=jnp.int32).reshape(dims)


def draw_pattern(key, part):
    coins = jax.random.randint(jax.random.fold_in(key, 21), (BOXES, NB, NB), 0, 5)
    stored = (coins < 3).astype(jnp.int32)
    eye_blocks = (jnp.arange(NB, dtype=jnp.int32)[:, None] == jnp.arange(NB, dtype=jnp.int32)[None, :]).astype(jnp.int32)
    return jnp.maximum(stored, eye_blocks[None, :, :])


def draw_shared(key, part):
    keys = jax.random.split(jax.random.fold_in(key, 31), BOXES)

    def pick(one_key):
        order = jax.random.permutation(one_key, NB)
        return jnp.sort(order[:NI]).astype(jnp.int32)
    return jax.vmap(pick)(keys)


def bell_draw(own_key, shape, width, limit, kind=jnp.bfloat16):
    values = width * jax.random.normal(own_key, shape, jnp.float32)
    return jnp.clip(values, min=-limit, max=limit).astype(kind)


def setup_inputs(seed: int = 0) -> dict:
    key_of = jax.random.split(jax.random.key(seed), 5)
    blocks = draw_blocks(jax.random.fold_in(key_of[4], 71), 0)
    pattern = draw_pattern(jax.random.fold_in(key_of[4], 71), 0)
    shared = draw_shared(jax.random.fold_in(key_of[4], 71), 0)
    sketch = bell_draw(key_of[3], (ORDER, COLS), 1.0, 6.0)
    return {"blocks": blocks, "pattern": pattern, "shared": shared, "sketch": sketch}


def one_box(box_blocks, box_pattern, box_shared, sketch_blocks):
    block_ids = jnp.arange(NB, dtype=jnp.int32)
    face_index = box_shared.astype(jnp.int32)
    chosen = face_index[:, None] == block_ids[None, :]
    exterior = 1 - jnp.any(chosen, axis=0).astype(jnp.int32)
    keep_ext = (box_pattern * exterior[None, :]).astype(box_blocks.dtype)
    kept_ext = (box_blocks * keep_ext[:, :, None, None]).astype(jnp.float32)
    sketched = jnp.einsum("ijpq,jqc->ipc", kept_ext, sketch_blocks.astype(jnp.float32), precision=lax.Precision.HIGHEST).astype(jnp.bfloat16)
    side_cols = box_blocks[:, face_index] * box_pattern[:, face_index].astype(box_blocks.dtype)[:, :, None, None]
    inner = side_cols[face_index]
    return sketched, side_cols, inner, face_index


def diagonal_of(inner):
    return jnp.diagonal(jnp.diagonal(inner, axis1=0, axis2=1), axis1=0, axis2=1).astype(jnp.float32)


def reference(blocks, pattern, shared, sketch):
    sketch_blocks = sketch.reshape(NB, BLK, COLS)
    pair_count = BOXES // 2

    def merge_pair(pair_index):
        first_box = (pair_index // BOX_DEV) * 2 * BOX_DEV + pair_index % BOX_DEV
        second_box = first_box + BOX_DEV
        outs = []
        parts = []
        for box_id in (first_box, second_box):
            parts.append(one_box(lax.dynamic_index_in_dim(blocks, box_id, 0, keepdims=False),
                                 lax.dynamic_index_in_dim(pattern, box_id, 0, keepdims=False),
                                 lax.dynamic_index_in_dim(shared, box_id, 0, keepdims=False),
                                 sketch_blocks))
        sketched_a, side_a, inner_a, index_a = parts[0]
        sketched_b, side_b, inner_b, index_b = parts[1]
        wide_a = lax.optimization_barrier(sketched_a).astype(jnp.float32)
        wide_b = lax.optimization_barrier(sketched_b).astype(jnp.float32)
        right_side = wide_a[index_a] + wide_b[index_b]
        diag_sum = diagonal_of(inner_a) + diagonal_of(inner_b)
        inner_fa = inner_a.astype(jnp.float32)
        inner_fb = inner_b.astype(jnp.float32)
        potential = right_side / diag_sum[:, :, None]
        for sweep_index in range(ITERS - 1):
            applied = jnp.einsum("klpq,lqc->kpc", inner_fa, potential, precision=lax.Precision.HIGHEST)
            applied = applied + jnp.einsum("klpq,lqc->kpc", inner_fb, potential, precision=lax.Precision.HIGHEST)
            potential = potential + (right_side - applied) / diag_sum[:, :, None]
        rounded = lax.optimization_barrier(potential.astype(jnp.bfloat16)).astype(jnp.float32)
        for wide, side_cols in ((wide_a, side_a), (wide_b, side_b)):
            correction = jnp.einsum("ikpq,kqc->ipc", side_cols.astype(jnp.float32), rounded, precision=lax.Precision.HIGHEST)
            outs.append((wide - correction).astype(jnp.bfloat16).reshape(NB * BLK, COLS))
        return jnp.stack(outs)

    result = lax.map(merge_pair, jnp.arange(pair_count, dtype=jnp.int32))
    result = result.reshape(N_BOX // 2, BOX_DEV, 2, NB * BLK, COLS)
    return jnp.transpose(result, (0, 2, 1, 3, 4)).reshape(BOXES, NB * BLK, COLS)
```

```python
import functools

import jax
import jax.numpy as jnp
from jax import lax
from jax.experimental import pallas as pl
from jax.experimental.pallas import tpu as pltpu
from jax.sharding import PartitionSpec as P

ITERS = 4
B = 128
MESH = pl.DeviceIdType.MESH
F32 = jnp.float32
B16 = jnp.bfloat16
ORDER = (2, 1, 3, 0)


def splat(scalar):
    return jnp.full((1, B), scalar.astype(F32), F32).astype(B16)


def kernel(
    blocks, pattern, shared, sketch, out,
    blk0, blk1, blk2, blk3, sk, am, yb, side, ost,
    s_keep, s_give, s_cin, s_ain, s_rin, s_t, s_sib, s_full, dinv,
    y_keep, y_give, y_cin, y_ain, y_rin, y_t, y_sib, pot_all,
    load_sem, out_sem, send_sem, recv_sem,
):
    blk = (blk0, blk1, blk2, blk3)
    box, face = lax.axis_index("box"), lax.axis_index("face")
    x, c = face // 2, face % 2
    other = 1 - c
    core_peer = (box, x * 2 + other)
    right = (box, ((x + 1) % 4) * 2 + c)
    left = (box, ((x + 3) % 4) * 2 + c)
    sibling = (box + 1 - 2 * (box % 2), face)
    used = [0]

    def send(src, dst, where):
        i = used[0]
        used[0] += 1
        copy = pltpu.make_async_remote_copy(
            src_ref=src, dst_ref=dst, send_sem=send_sem.at[i], recv_sem=recv_sem.at[i],
            device_id=where, device_id_type=MESH,
        )
        copy.start()
        return copy

    sent = []

    def go(src, dst, where):
        copy = send(src, dst, where)
        sent.append(copy)
        return copy

    box_of = [(x + q) % 4 for q in range(4)]
    loads = {}
    for n, q in enumerate(ORDER):
        loads[q] = pltpu.make_async_copy(blocks.at[box_of[q]], blk[q], load_sem.at[n])
        loads[q].start()
        if n == 0:
            load_sk = pltpu.make_async_copy(sketch, sk, load_sem.at[4])
            load_sk.start()

    barrier = pltpu.get_barrier_semaphore()
    for peer in (core_peer, right, left, sibling):
        pl.semaphore_signal(barrier, inc=1, device_id=peer, device_id_type=MESH)
    pl.semaphore_wait(barrier, 4)

    def slot(q, k):
        r = shared[box_of[q], k] - 3 * face
        own = jnp.where(jnp.logical_and(r >= 0, r < 3), 1, 0)
        return own, jnp.clip(r, 0, 2)

    def take_s(q):
        @pl.loop(0, 4)
        def _(k):
            own, r = slot(q, k)
            for half, ref in ((other, s_give), (c, s_keep)):
                for l in range(2):
                    j = shared[box_of[q], 2 * half + l]
                    w = own * pattern[r, box_of[q], j]
                    ref[q, pl.ds(k * B, B), l * B:(l + 1) * B] = blk[q][r * 24 + j] * splat(w)

    def sketch_rows(q):
        b = box_of[q]

        @pl.loop(0, 24)
        def _(j):
            inner = jnp.int32(0)
            for k in range(4):
                inner = inner + jnp.where(shared[b, k] == j, 1, 0)
            for r in range(3):
                w = (1 - inner) * pattern[r, b, j]
                am[r * B:(r + 1) * B, pl.ds(pl.multiple_of(j * B, B), B)] = blk[q][r * 24 + j] * splat(w)

        acc = jnp.dot(am[...], sk[...], preferred_element_type=F32).astype(B16)
        for r in range(3):
            for h in range(2):
                yb[q, h, r] = acc[r * B:(r + 1) * B, h * B:(h + 1) * B]

        @pl.loop(0, 4)
        def _(k):
            own, r = slot(q, k)
            w = splat(own)
            y_give[q, pl.ds(k * B, B), :] = yb[q, other, r] * w
            y_keep[q, pl.ds(k * B, B), :] = yb[q, c, r] * w

    def take_side(q):
        b = box_of[q]

        @pl.loop(0, 3)
        def _(r):
            for l in range(4):
                j = shared[b, l]
                side[q, pl.ds(r * B, B), l * B:(l + 1) * B] = blk[q][r * 24 + j] * splat(pattern[r, b, j])

    h0, h1 = pl.ds(0, 256), pl.ds(256, 256)

    def core_swap(give, cin, q):
        return go(give.at[q], cin.at[q], core_peer)

    def core_merge(keep, cin, q, copy):
        copy.wait_recv()
        keep[q] = keep[q] + cin[q]

    s_core = {}
    for q in ORDER:
        loads[q].wait()
        take_s(q)
        s_core[q] = core_swap(s_give, s_cin, q)
    load_sk.wait()
    y_core = {}

    def first_hops(keep, cin, ain, rin, core):
        core_merge(keep, cin, 2, core[2])
        a_right = go(keep.at[2, h0], ain.at[0], right)
        a_left = go(keep.at[2, h1], ain.at[1], left)
        core_merge(keep, cin, 1, core[1])
        b_right = go(keep.at[1, h1], rin.at[0, h1], right)
        core_merge(keep, cin, 3, core[3])
        b_left = go(keep.at[3, h0], rin.at[1, h0], left)
        return a_right, a_left, b_right, b_left

    def second_hops(keep, ain, rin, a_right, a_left):
        a_right.wait_recv()
        keep[1, h0] = keep[1, h0] + ain[0]
        c_right = go(keep.at[1, h0], rin.at[0, h0], right)
        a_left.wait_recv()
        keep[3, h1] = keep[3, h1] + ain[1]
        c_left = go(keep.at[3, h1], rin.at[1, h1], left)
        return c_right, c_left

    def to_sibling(keep, rin, t, sib, b_right, b_left, c_right, c_left):
        for copy in (b_right, b_left, c_right, c_left):
            copy.wait_recv()
        t[...] = keep[0] + rin[0] + rin[1]
        return go(t, sib, sibling)

    sketch_rows(2)
    y_core[2] = core_swap(y_give, y_cin, 2)
    s_hops = first_hops(s_keep, s_cin, s_ain, s_rin, s_core)
    sketch_rows(1)
    y_core[1] = core_swap(y_give, y_cin, 1)
    sketch_rows(3)
    y_core[3] = core_swap(y_give, y_cin, 3)
    s_more = second_hops(s_keep, s_ain, s_rin, s_hops[0], s_hops[1])
    sketch_rows(0)
    y_core[0] = core_swap(y_give, y_cin, 0)
    y_hops = first_hops(y_keep, y_cin, y_ain, y_rin, y_core)
    core_merge(s_keep, s_cin, 0, s_core[0])
    core_merge(y_keep, y_cin, 0, y_core[0])
    for q in ORDER:
        take_side(q)
    s_pair = to_sibling(s_keep, s_rin, s_t, s_sib, s_hops[2], s_hops[3], *s_more)
    y_more = second_hops(y_keep, y_ain, y_rin, y_hops[0], y_hops[1])

    s_pair.wait_recv()
    eye = lax.broadcasted_iota(jnp.int32, (B, B), 0) == lax.broadcasted_iota(jnp.int32, (B, B), 1)
    s_full[c] = (s_t[...].astype(F32) + s_sib[...].astype(F32)).astype(B16)
    for l in range(2):
        rows = pl.ds(pl.multiple_of((2 * c + l) * B, B), B)
        cols = slice(l * B, (l + 1) * B)
        both = s_t[rows, cols].astype(F32) + s_sib[rows, cols].astype(F32)
        d = jnp.sum(jnp.where(eye, both, 0.0), axis=1, keepdims=True)
        dinv[c, l * B:(l + 1) * B, :] = jnp.broadcast_to(1.0 / d, (B, B))
        s_full[c, rows, cols] = jnp.where(eye, 0.0, both).astype(B16)
    s_half = go(s_full.at[c], s_full.at[c], core_peer)
    d_half = go(dinv.at[c], dinv.at[c], core_peer)

    y_pair = to_sibling(y_keep, y_rin, y_t, y_sib, y_hops[2], y_hops[3], *y_more)
    s_half.wait_recv()
    d_half.wait_recv()
    y_pair.wait_recv()

    rhs = y_t[...].astype(F32) + y_sib[...].astype(F32)
    scale = dinv[...].reshape(4 * B, B)
    pot = rhs * scale
    for _ in range(ITERS - 1):
        upper = pot.astype(B16)
        lower = (pot - upper.astype(F32)).astype(B16)
        both = jnp.concatenate([upper, lower], axis=1)
        terms = jnp.dot(s_full[0], both[:256], preferred_element_type=F32)
        terms = terms + jnp.dot(s_full[1], both[256:], preferred_element_type=F32)
        pot = (rhs - (terms[:, :B] + terms[:, B:])) * scale
    pot_all[0, c] = pot.astype(B16)

    def correct(q, n):
        both = jnp.concatenate([pot_all[q, 0], pot_all[q, 1]], axis=1)
        corr = jnp.dot(side[q], both, preferred_element_type=F32)
        for r in range(3):
            for h in range(2):
                rows, cols = slice(r * B, (r + 1) * B), slice(h * B, (h + 1) * B)
                ost[q, rows, cols] = (yb[q, h, r].astype(F32) - corr[rows, cols]).astype(B16)
        copy = pltpu.make_async_copy(ost.at[q], out.at[box_of[q]], out_sem.at[n])
        copy.start()
        return copy

    mine = pot_all.at[0, c]
    p_right = go(mine, pot_all.at[3, c], right)
    p_left = go(mine, pot_all.at[1, c], left)
    p_core = go(mine, mine, core_peer)
    p_right.wait_recv()
    f_right = go(pot_all.at[3, c, h0], pot_all.at[2, c, h0], right)
    c3 = go(pot_all.at[3, c], pot_all.at[3, c], core_peer)
    p_left.wait_recv()
    f_left = go(pot_all.at[1, c, h1], pot_all.at[2, c, h1], left)
    c1 = go(pot_all.at[1, c], pot_all.at[1, c], core_peer)
    outs = []
    p_core.wait_recv()
    outs.append(correct(0, 0))
    c3.wait_recv()
    outs.append(correct(3, 1))
    c1.wait_recv()
    outs.append(correct(1, 2))
    f_right.wait_recv()
    e0 = go(pot_all.at[2, c, h0], pot_all.at[2, c, h0], core_peer)
    f_left.wait_recv()
    e1 = go(pot_all.at[2, c, h1], pot_all.at[2, c, h1], core_peer)
    e0.wait_recv()
    e1.wait_recv()
    outs.append(correct(2, 3))
    for copy in sent:
        copy.wait_send()
    for copy in outs:
        copy.wait()


N_COPIES = 34


def local(blocks, pattern, shared, sketch):
    boxes, rows, cols, blk, _ = blocks.shape
    order, width = sketch.shape
    blocks = blocks.reshape(boxes, rows * cols, blk, blk)
    pattern = pattern.transpose(1, 0, 2)
    v = pltpu.VMEM
    return pl.pallas_call(
        kernel,
        out_shape=jax.ShapeDtypeStruct((boxes, rows * blk, width), B16),
        in_specs=[
            pl.BlockSpec(memory_space=pl.ANY),
            pl.BlockSpec(memory_space=pltpu.SMEM),
            pl.BlockSpec(memory_space=pltpu.SMEM),
            pl.BlockSpec(memory_space=pl.ANY),
        ],
        out_specs=pl.BlockSpec(memory_space=pl.ANY),
        scratch_shapes=[
            *[v((rows * cols, blk, blk), B16) for _ in range(4)],
            v((order, width), B16),
            v((rows * blk, order), B16),
            v((4, 2, rows, blk, blk), B16),
            v((4, rows * blk, 512), B16),
            v((4, rows * blk, width), B16),
            v((4, 512, 256), B16), v((4, 512, 256), B16), v((4, 512, 256), B16),
            v((2, 256, 256), B16), v((2, 512, 256), B16), v((512, 256), B16), v((512, 256), B16),
            v((2, 512, 256), B16), v((2, 256, 128), F32),
            v((4, 512, 128), B16), v((4, 512, 128), B16), v((4, 512, 128), B16),
            v((2, 256, 128), B16), v((2, 512, 128), B16), v((512, 128), B16), v((512, 128), B16),
            v((4, 2, 512, 128), B16),
            pltpu.SemaphoreType.DMA((5,)),
            pltpu.SemaphoreType.DMA((4,)),
            pltpu.SemaphoreType.DMA((N_COPIES,)),
            pltpu.SemaphoreType.DMA((N_COPIES,)),
        ],
        compiler_params=pltpu.CompilerParams(
            collective_id=0, has_side_effects=True, vmem_limit_bytes=62_400_000
        ),
        cost_estimate=pl.CostEstimate(flops=3_300_000_000, bytes_accessed=12_000_000, transcendentals=0),
    )(blocks, pattern, shared, sketch)


def solution(mesh):
    return jax.shard_map(
        local,
        mesh=mesh,
        in_specs=(P("box", "face", None, None, None), P("box", "face", None), P("box", None), P()),
        out_specs=P("box", "face", None),
        check_vma=False,
    )
```

```python
import functools

import jax
import jax.numpy as jnp
from jax import lax
from jax.experimental import pallas as pl
from jax.experimental.pallas import tpu as pltpu
from jax.sharding import PartitionSpec as P

ITERS = 4
B = 128
MESH = pl.DeviceIdType.MESH
F32 = jnp.float32
B16 = jnp.bfloat16
ORDER = (2, 1, 3, 0)


def splat(scalar):
    return jnp.full((1, B), scalar.astype(F32), F32).astype(B16)


def kernel(
    blocks, pattern, shared, sketch, out,
    blk0, blk1, blk2, blk3, sk, am, yb, side,
    keep, give, cin, ain, rin, total, sib, s_full, dinv, pot_all,
    load_sem, send_sem, recv_sem,
):
    blk = (blk0, blk1, blk2, blk3)
    box, face = lax.axis_index("box"), lax.axis_index("face")
    x, c = face // 2, face % 2
    other = 1 - c
    core_peer = (box, x * 2 + other)
    right = (box, ((x + 1) % 4) * 2 + c)
    left = (box, ((x + 3) % 4) * 2 + c)
    sibling = (box + 1 - 2 * (box % 2), face)
    sent = []

    def go(src, dst, where):
        i = len(sent)
        copy = pltpu.make_async_remote_copy(
            src_ref=src, dst_ref=dst, send_sem=send_sem.at[i], recv_sem=recv_sem.at[i],
            device_id=where, device_id_type=MESH,
        )
        copy.start()
        sent.append(copy)
        return copy

    box_of = [(x + q) % 4 for q in range(4)]
    loads = {
        q: pltpu.make_async_copy(blocks.at[box_of[q]], blk[q], load_sem.at[q]) for q in range(4)
    }
    load_sk = pltpu.make_async_copy(sketch, sk, load_sem.at[4])
    loads[2].start()
    loads[1].start()

    barrier = pltpu.get_barrier_semaphore()
    for peer in (core_peer, right, left, sibling):
        pl.semaphore_signal(barrier, inc=1, device_id=peer, device_id_type=MESH)

    def slot(q, k):
        r = shared[box_of[q], k] - 3 * face
        own = jnp.where(jnp.logical_and(r >= 0, r < 3), 1, 0)
        return own, jnp.clip(r, 0, 2)

    def take_s(q):
        @pl.loop(0, 4)
        def _(k):
            own, r = slot(q, k)
            for half, ref in ((other, give), (c, keep)):
                for t in range(2):
                    j = shared[box_of[q], 2 * half + t]
                    w = own * pattern[r, box_of[q], j]
                    ref[t, q, pl.ds(k * B, B), :] = blk[q][r * 24 + j] * splat(w)

    def sketch_rows(q):
        b = box_of[q]

        inner = [shared[b, k] for k in range(4)]
        for j in range(24):
            ext = jnp.int32(1)
            for k in range(4):
                ext = ext * jnp.where(inner[k] == j, 0, 1)
            for r in range(3):
                w = splat(ext * pattern[r, b, j])
                am[r * B:(r + 1) * B, j * B:(j + 1) * B] = blk[q][r * 24 + j] * w

        acc = jnp.dot(am[...], sk[...], preferred_element_type=F32).astype(B16)
        for r in range(3):
            for h in range(2):
                yb[q, h, r] = acc[r * B:(r + 1) * B, h * B:(h + 1) * B]

        @pl.loop(0, 4)
        def _(k):
            own, r = slot(q, k)
            w = splat(own)
            give[2, q, pl.ds(k * B, B), :] = yb[q, other, r] * w
            keep[2, q, pl.ds(k * B, B), :] = yb[q, c, r] * w

    def take_side(q):
        b = box_of[q]

        @pl.loop(0, 3)
        def _(r):
            for l in range(4):
                j = shared[b, l]
                side[q, pl.ds(r * B, B), l * B:(l + 1) * B] = blk[q][r * 24 + j] * splat(pattern[r, b, j])

    swaps = {}

    def swap(t, q):
        swaps[t, q] = go(give.at[t, q], cin.at[t, q], core_peer)

    def merge(t, q):
        swaps[t, q].wait_recv()
        keep[t, q] = keep[t, q] + cin[t, q]

    jobs = [
        (0, (0, 256), (256, 256)),
        (1, (0, 256), (256, 256)),
        (2, (0, 128), (256, 128)),
        (2, (128, 128), (384, 128)),
    ]
    hops = {}

    def hop_a(n):
        t, h0, h1 = jobs[n]
        h0, h1 = pl.ds(*h0), pl.ds(*h1)
        hops["ar", n] = go(keep.at[t, 2, h0], ain.at[t, h0], right)
        hops["al", n] = go(keep.at[t, 2, h1], ain.at[t, h1], left)

    def hop_b(n):
        t, h0, h1 = jobs[n]
        h0, h1 = pl.ds(*h0), pl.ds(*h1)
        hops["br", n] = go(keep.at[t, 1, h1], rin.at[t, 0, h1], right)
        hops["bl", n] = go(keep.at[t, 3, h0], rin.at[t, 1, h0], left)

    def hop_c(n):
        t, h0, h1 = jobs[n]
        h0, h1 = pl.ds(*h0), pl.ds(*h1)
        hops["ar", n].wait_recv()
        keep[t, 1, h0] = keep[t, 1, h0] + ain[t, h0]
        hops["cr", n] = go(keep.at[t, 1, h0], rin.at[t, 0, h0], right)
        hops["al", n].wait_recv()
        keep[t, 3, h1] = keep[t, 3, h1] + ain[t, h1]
        hops["cl", n] = go(keep.at[t, 3, h1], rin.at[t, 1, h1], left)

    def to_sibling(n):
        t, h0, h1 = jobs[n]
        hops["s", n] = []
        for h, need in ((pl.ds(*h0), ("bl", "cr")), (pl.ds(*h1), ("br", "cl"))):
            for name in need:
                hops[name, n].wait_recv()
            total[t, h] = keep[t, 0, h] + rin[t, 0, h] + rin[t, 1, h]
            hops["s", n].append(go(total.at[t, h], sib.at[t, h], sibling))

    eye = lax.broadcasted_iota(jnp.int32, (B, B), 0) == lax.broadcasted_iota(jnp.int32, (B, B), 1)

    def sum_pair(t):
        for copy in hops["s", t]:
            copy.wait_recv()
        place = 2 * c + t
        s_full[place] = (total[t].astype(F32) + sib[t].astype(F32)).astype(B16)
        rows = pl.ds(pl.multiple_of(place * B, B), B)
        both = total[t, rows].astype(F32) + sib[t, rows].astype(F32)
        d = jnp.sum(jnp.where(eye, both, 0.0), axis=1, keepdims=True)
        dinv[place] = jnp.broadcast_to(1.0 / d, (B, B))
        s_full[place, rows] = jnp.where(eye, 0.0, both).astype(B16)
        return (
            go(s_full.at[place], s_full.at[place], core_peer),
            go(dinv.at[place], dinv.at[place], core_peer),
        )

    loads[2].wait()
    loads[3].start()
    take_s(2)
    pl.semaphore_wait(barrier, 4)
    swap(0, 2)
    swap(1, 2)
    loads[1].wait()
    loads[0].start()
    load_sk.start()
    take_s(1)
    swap(0, 1)
    merge(0, 2)
    hop_a(0)
    swap(1, 1)
    loads[3].wait()
    take_s(3)
    swap(0, 3)
    swap(1, 3)
    merge(0, 1)
    merge(0, 3)
    hop_b(0)
    merge(1, 2)
    hop_a(1)
    merge(1, 1)
    merge(1, 3)
    loads[0].wait()
    take_s(0)
    swap(0, 0)
    swap(1, 0)
    load_sk.wait()
    sketch_rows(2)
    swap(2, 2)
    hop_c(0)
    hop_b(1)
    merge(0, 0)
    merge(1, 0)
    sketch_rows(1)
    swap(2, 1)
    hop_c(1)
    sketch_rows(3)
    swap(2, 3)
    merge(2, 2)
    hop_a(2)
    hop_a(3)
    to_sibling(0)
    merge(2, 1)
    merge(2, 3)
    hop_b(2)
    sketch_rows(0)
    swap(2, 0)
    to_sibling(1)
    hop_c(2)
    hop_b(3)
    merge(2, 0)
    for q in ORDER:
        take_side(q)
    halves = [*sum_pair(0)]
    hop_c(3)
    to_sibling(2)
    to_sibling(3)
    halves += sum_pair(1)
    for copy in hops["s", 2] + hops["s", 3] + halves:
        copy.wait_recv()

    rhs = total[2].astype(F32) + sib[2].astype(F32)
    scale = dinv[...].reshape(4 * B, B)
    wide = jnp.concatenate([s_full[l] for l in range(4)], axis=1)
    pot = rhs * scale
    for _ in range(ITERS - 1):
        upper = pot.astype(B16)
        lower = (pot - upper.astype(F32)).astype(B16)
        terms = jnp.dot(wide, jnp.concatenate([upper, lower], axis=1), preferred_element_type=F32)
        pot = (rhs - (terms[:, :B] + terms[:, B:])) * scale
    pot_all[0, c] = pot.astype(B16)

    def correct(q, h):
        corr = jnp.dot(side[q], pot_all[q, h], preferred_element_type=F32)
        cols = pl.ds(pl.multiple_of(h * B, B), B)
        for r in range(3):
            rows = slice(r * B, (r + 1) * B)
            out[box_of[q], rows, cols] = (yb[q, h, r].astype(F32) - corr[rows]).astype(B16)

    top, low = pl.ds(0, 256), pl.ds(256, 256)

    def pass_on(q, h, where, to):
        return go(pot_all.at[q, c, h], pot_all.at[to, c, h], where)

    p3t = pass_on(0, top, right, 3)
    p1l = pass_on(0, low, left, 1)
    p3l = pass_on(0, low, right, 3)
    p1t = pass_on(0, top, left, 1)
    own = go(pot_all.at[0, c], pot_all.at[0, c], core_peer)
    correct(0, c)
    p3t.wait_recv()
    f2t = pass_on(3, top, right, 2)
    p1l.wait_recv()
    f2l = pass_on(1, low, left, 2)
    own.wait_recv()
    correct(0, other)
    p3l.wait_recv()
    e3 = go(pot_all.at[3, c], pot_all.at[3, c], core_peer)
    p1t.wait_recv()
    e1 = go(pot_all.at[1, c], pot_all.at[1, c], core_peer)
    correct(3, c)
    correct(1, c)
    f2t.wait_recv()
    e2t = pass_on(2, top, core_peer, 2)
    f2l.wait_recv()
    e2l = pass_on(2, low, core_peer, 2)
    e3.wait_recv()
    correct(3, other)
    e1.wait_recv()
    correct(1, other)
    correct(2, c)
    e2t.wait_recv()
    e2l.wait_recv()
    correct(2, other)
    for copy in sent:
        copy.wait_send()


N_COPIES = 64


def local(blocks, pattern, shared, sketch):
    boxes, rows, cols, blk, _ = blocks.shape
    order, width = sketch.shape
    blocks = blocks.reshape(boxes, rows * cols, blk, blk)
    pattern = pattern.transpose(1, 0, 2)
    v = pltpu.VMEM
    return pl.pallas_call(
        kernel,
        out_shape=v((boxes, rows * blk, width), B16),
        in_specs=[
            pl.BlockSpec(memory_space=pltpu.HBM),
            pl.BlockSpec(memory_space=pltpu.SMEM),
            pl.BlockSpec(memory_space=pltpu.SMEM),
            pl.BlockSpec(memory_space=pltpu.HBM),
        ],
        out_specs=pl.BlockSpec(memory_space=pltpu.VMEM),
        scratch_shapes=[
            *[v((rows * cols, blk, blk), B16) for _ in range(4)],
            v((order, width), B16),
            v((rows * blk, order), B16),
            v((4, 2, rows, blk, blk), B16),
            v((4, rows * blk, 512), B16),
            v((3, 4, 512, 128), B16), v((3, 4, 512, 128), B16), v((3, 4, 512, 128), B16),
            v((3, 512, 128), B16), v((3, 2, 512, 128), B16), v((3, 512, 128), B16), v((3, 512, 128), B16),
            v((4, 512, 128), B16), v((4, 128, 128), F32), v((4, 2, 512, 128), B16),
            pltpu.SemaphoreType.DMA((5,)),
            pltpu.SemaphoreType.DMA((N_COPIES,)),
            pltpu.SemaphoreType.DMA((N_COPIES,)),
        ],
        compiler_params=pltpu.CompilerParams(
            collective_id=0, has_side_effects=True, vmem_limit_bytes=56_000_000
        ),
        cost_estimate=pl.CostEstimate(flops=3_300_000_000, bytes_accessed=12_000_000, transcendentals=0),
    )(blocks, pattern, shared, sketch)


def solution(mesh):
    return jax.shard_map(
        local,
        mesh=mesh,
        in_specs=(P("box", "face", None, None, None), P("box", "face", None), P("box", None), P()),
        out_specs=P("box", "face", None),
        check_vma=False,
    )
```

```python
import functools

import jax
import jax.numpy as jnp
from jax import lax
from jax.experimental import pallas as pl
from jax.experimental.pallas import tpu as pltpu
from jax.sharding import PartitionSpec as P

ITERS = 4
B = 128
MESH = pl.DeviceIdType.MESH
F32 = jnp.float32
B16 = jnp.bfloat16
ORDER = (2, 1, 3, 0)


def splat(scalar):
    return jnp.full((1, B), scalar.astype(F32), F32).astype(B16)


def kernel(
    blocks, pattern, shared, sketch, out,
    blk0, blk1, blk2, blk3, sk, am, yb, side,
    keep, give, cin, ain, rin, total, sib, s_full, dinv, pot_all,
    load_sem, send_sem, recv_sem,
):
    blk = (blk0, blk1, blk2, blk3)
    box, face = lax.axis_index("box"), lax.axis_index("face")
    x, c = face // 2, face % 2
    other = 1 - c
    core_peer = (box, x * 2 + other)
    right = (box, ((x + 1) % 4) * 2 + c)
    left = (box, ((x + 3) % 4) * 2 + c)
    sibling = (box + 1 - 2 * (box % 2), face)
    sent = []

    def go(src, dst, where):
        i = len(sent)
        copy = pltpu.make_async_remote_copy(
            src_ref=src, dst_ref=dst, send_sem=send_sem.at[i], recv_sem=recv_sem.at[i],
            device_id=where, device_id_type=MESH,
        )
        copy.start()
        sent.append(copy)
        return copy

    box_of = [(x + q) % 4 for q in range(4)]
    loads = {
        q: pltpu.make_async_copy(blocks.at[box_of[q]], blk[q], load_sem.at[q]) for q in range(4)
    }
    load_sk = pltpu.make_async_copy(sketch, sk, load_sem.at[4])
    loads[2].start()
    loads[1].start()
    loads[3].start()
    loads[0].start()
    load_sk.start()

    barrier = pltpu.get_barrier_semaphore()
    for peer in (core_peer, right, left, sibling):
        pl.semaphore_signal(barrier, inc=1, device_id=peer, device_id_type=MESH)

    def slot(q, k):
        r = shared[box_of[q], k] - 3 * face
        own = jnp.where(jnp.logical_and(r >= 0, r < 3), 1, 0)
        return own, jnp.clip(r, 0, 2)

    def take_s(q):
        @pl.loop(0, 4)
        def _(k):
            own, r = slot(q, k)
            for half, ref in ((other, give), (c, keep)):
                for t in range(2):
                    j = shared[box_of[q], 2 * half + t]
                    w = own * pattern[r, box_of[q], j]
                    ref[t, q, pl.ds(k * B, B), :] = blk[q][r * 24 + j] * splat(w)

    def sketch_rows(q):
        b = box_of[q]

        inner = [shared[b, k] for k in range(4)]
        for j in range(24):
            ext = jnp.int32(1)
            for k in range(4):
                ext = ext * jnp.where(inner[k] == j, 0, 1)
            for r in range(3):
                w = splat(ext * pattern[r, b, j])
                am[r * B:(r + 1) * B, j * B:(j + 1) * B] = blk[q][r * 24 + j] * w

        acc = jnp.dot(am[...], sk[...], preferred_element_type=F32).astype(B16)
        for r in range(3):
            for h in range(2):
                yb[q, h, r] = acc[r * B:(r + 1) * B, h * B:(h + 1) * B]

        @pl.loop(0, 4)
        def _(k):
            own, r = slot(q, k)
            w = splat(own)
            give[2, q, pl.ds(k * B, B), :] = yb[q, other, r] * w
            keep[2, q, pl.ds(k * B, B), :] = yb[q, c, r] * w

    def take_side(q):
        b = box_of[q]

        @pl.loop(0, 3)
        def _(r):
            for l in range(4):
                j = shared[b, l]
                side[q, pl.ds(r * B, B), l * B:(l + 1) * B] = blk[q][r * 24 + j] * splat(pattern[r, b, j])

    swaps = {}

    def swap(t, q):
        swaps[t, q] = go(give.at[t, q], cin.at[t, q], core_peer)

    def merge(t, q):
        swaps[t, q].wait_recv()
        keep[t, q] = keep[t, q] + cin[t, q]

    jobs = [
        (0, (0, 256), (256, 256)),
        (1, (0, 256), (256, 256)),
        (2, (0, 128), (256, 128)),
        (2, (128, 128), (384, 128)),
    ]
    hops = {}

    def hop_a(n):
        t, h0, h1 = jobs[n]
        h0, h1 = pl.ds(*h0), pl.ds(*h1)
        hops["ar", n] = go(keep.at[t, 2, h0], ain.at[t, h0], right)
        hops["al", n] = go(keep.at[t, 2, h1], ain.at[t, h1], left)

    def hop_b(n):
        t, h0, h1 = jobs[n]
        h0, h1 = pl.ds(*h0), pl.ds(*h1)
        hops["br", n] = go(keep.at[t, 1, h1], rin.at[t, 0, h1], right)
        hops["bl", n] = go(keep.at[t, 3, h0], rin.at[t, 1, h0], left)

    def hop_c(n):
        t, h0, h1 = jobs[n]
        h0, h1 = pl.ds(*h0), pl.ds(*h1)
        hops["ar", n].wait_recv()
        keep[t, 1, h0] = keep[t, 1, h0] + ain[t, h0]
        hops["cr", n] = go(keep.at[t, 1, h0], rin.at[t, 0, h0], right)
        hops["al", n].wait_recv()
        keep[t, 3, h1] = keep[t, 3, h1] + ain[t, h1]
        hops["cl", n] = go(keep.at[t, 3, h1], rin.at[t, 1, h1], left)

    def to_sibling(n):
        t, h0, h1 = jobs[n]
        hops["s", n] = []
        for h, need in ((pl.ds(*h0), ("bl", "cr")), (pl.ds(*h1), ("br", "cl"))):
            for name in need:
                hops[name, n].wait_recv()
            total[t, h] = keep[t, 0, h] + rin[t, 0, h] + rin[t, 1, h]
            hops["s", n].append(go(total.at[t, h], sib.at[t, h], sibling))

    eye = lax.broadcasted_iota(jnp.int32, (B, B), 0) == lax.broadcasted_iota(jnp.int32, (B, B), 1)

    def sum_pair(t):
        for copy in hops["s", t]:
            copy.wait_recv()
        place = 2 * c + t
        s_full[place] = (total[t].astype(F32) + sib[t].astype(F32)).astype(B16)
        rows = pl.ds(pl.multiple_of(place * B, B), B)
        both = total[t, rows].astype(F32) + sib[t, rows].astype(F32)
        d = jnp.sum(jnp.where(eye, both, 0.0), axis=1, keepdims=True)
        dinv[place] = jnp.broadcast_to(1.0 / d, (B, B))
        s_full[place, rows] = jnp.where(eye, 0.0, both).astype(B16)
        return (
            go(s_full.at[place], s_full.at[place], core_peer),
            go(dinv.at[place], dinv.at[place], core_peer),
        )

    loads[2].wait()
    take_s(2)
    pl.semaphore_wait(barrier, 4)
    swap(0, 2)
    loads[1].wait()
    take_s(1)
    swap(0, 1)
    merge(0, 2)
    hop_a(0)
    loads[3].wait()
    take_s(3)
    swap(0, 3)
    swap(1, 2)
    merge(0, 1)
    merge(0, 3)
    hop_b(0)
    swap(1, 1)
    swap(1, 3)
    merge(1, 2)
    hop_a(1)
    merge(1, 1)
    merge(1, 3)
    loads[0].wait()
    take_s(0)
    swap(0, 0)
    swap(1, 0)
    load_sk.wait()
    sketch_rows(2)
    swap(2, 2)
    hop_c(0)
    hop_b(1)
    merge(0, 0)
    merge(1, 0)
    sketch_rows(1)
    swap(2, 1)
    hop_c(1)
    sketch_rows(3)
    swap(2, 3)
    merge(2, 2)
    hop_a(2)
    hop_a(3)
    to_sibling(0)
    merge(2, 1)
    merge(2, 3)
    hop_b(2)
    sketch_rows(0)
    swap(2, 0)
    to_sibling(1)
    hop_c(2)
    hop_b(3)
    merge(2, 0)
    for q in ORDER:
        take_side(q)
    halves = [*sum_pair(0)]
    hop_c(3)
    to_sibling(2)
    to_sibling(3)
    halves += sum_pair(1)
    for copy in hops["s", 2] + hops["s", 3] + halves:
        copy.wait_recv()

    rhs = total[2].astype(F32) + sib[2].astype(F32)
    scale = dinv[...].reshape(4 * B, B)
    wide = jnp.concatenate([s_full[l] for l in range(4)], axis=1)
    pot = rhs * scale
    for _ in range(ITERS - 1):
        upper = pot.astype(B16)
        lower = (pot - upper.astype(F32)).astype(B16)
        terms = jnp.dot(wide, jnp.concatenate([upper, lower], axis=1), preferred_element_type=F32)
        pot = (rhs - (terms[:, :B] + terms[:, B:])) * scale
    pot_all[0, c] = pot.astype(B16)

    def correct(q, h):
        corr = jnp.dot(side[q], pot_all[q, h], preferred_element_type=F32)
        cols = pl.ds(pl.multiple_of(h * B, B), B)
        for r in range(3):
            rows = slice(r * B, (r + 1) * B)
            out[box_of[q], rows, cols] = (yb[q, h, r].astype(F32) - corr[rows]).astype(B16)

    top, low = pl.ds(0, 256), pl.ds(256, 256)

    def pass_on(q, h, where, to):
        return go(pot_all.at[q, c, h], pot_all.at[to, c, h], where)

    p3t = pass_on(0, top, right, 3)
    p1l = pass_on(0, low, left, 1)
    p3l = pass_on(0, low, right, 3)
    p1t = pass_on(0, top, left, 1)
    own = go(pot_all.at[0, c], pot_all.at[0, c], core_peer)
    correct(0, c)
    p3t.wait_recv()
    f2t = pass_on(3, top, right, 2)
    p1l.wait_recv()
    f2l = pass_on(1, low, left, 2)
    own.wait_recv()
    correct(0, other)
    p3l.wait_recv()
    e3 = go(pot_all.at[3, c], pot_all.at[3, c], core_peer)
    p1t.wait_recv()
    e1 = go(pot_all.at[1, c], pot_all.at[1, c], core_peer)
    correct(3, c)
    correct(1, c)
    f2t.wait_recv()
    e2t = pass_on(2, top, core_peer, 2)
    f2l.wait_recv()
    e2l = pass_on(2, low, core_peer, 2)
    e3.wait_recv()
    correct(3, other)
    e1.wait_recv()
    correct(1, other)
    correct(2, c)
    e2t.wait_recv()
    e2l.wait_recv()
    correct(2, other)
    for copy in sent:
        copy.wait_send()


N_COPIES = 64


def local(blocks, pattern, shared, sketch):
    boxes, rows, cols, blk, _ = blocks.shape
    order, width = sketch.shape
    blocks = blocks.reshape(boxes, rows * cols, blk, blk)
    pattern = pattern.transpose(1, 0, 2)
    v = pltpu.VMEM
    return pl.pallas_call(
        kernel,
        out_shape=v((boxes, rows * blk, width), B16),
        in_specs=[
            pl.BlockSpec(memory_space=pltpu.HBM),
            pl.BlockSpec(memory_space=pltpu.SMEM),
            pl.BlockSpec(memory_space=pltpu.SMEM),
            pl.BlockSpec(memory_space=pltpu.HBM),
        ],
        out_specs=pl.BlockSpec(memory_space=pltpu.VMEM),
        scratch_shapes=[
            *[v((rows * cols, blk, blk), B16) for _ in range(4)],
            v((order, width), B16),
            v((rows * blk, order), B16),
            v((4, 2, rows, blk, blk), B16),
            v((4, rows * blk, 512), B16),
            v((3, 4, 512, 128), B16), v((3, 4, 512, 128), B16), v((3, 4, 512, 128), B16),
            v((3, 512, 128), B16), v((3, 2, 512, 128), B16), v((3, 512, 128), B16), v((3, 512, 128), B16),
            v((4, 512, 128), B16), v((4, 128, 128), F32), v((4, 2, 512, 128), B16),
            pltpu.SemaphoreType.DMA((5,)),
            pltpu.SemaphoreType.DMA((N_COPIES,)),
            pltpu.SemaphoreType.DMA((N_COPIES,)),
        ],
        compiler_params=pltpu.CompilerParams(
            collective_id=0, has_side_effects=True, vmem_limit_bytes=56_000_000
        ),
        cost_estimate=pl.CostEstimate(flops=3_300_000_000, bytes_accessed=12_000_000, transcendentals=0),
    )(blocks, pattern, shared, sketch)


def solution(mesh):
    return jax.shard_map(
        local,
        mesh=mesh,
        in_specs=(P("box", "face", None, None, None), P("box", "face", None), P("box", None), P()),
        out_specs=P("box", "face", None),
        check_vma=False,
    )
```

```python
import functools

import jax
import jax.numpy as jnp
from jax import lax
from jax.experimental import pallas as pl
from jax.experimental.pallas import tpu as pltpu
from jax.sharding import PartitionSpec as P

ITERS = 4
B = 128
MESH = pl.DeviceIdType.MESH
F32 = jnp.float32
B16 = jnp.bfloat16
ORDER = (2, 1, 3, 0)


def splat(scalar):
    return jnp.full((1, B), scalar.astype(F32), F32).astype(B16)


def kernel(
    blocks, pattern, shared, sketch, out,
    blk0, blk1, blk2, blk3, sk, am, yb, side,
    keep, give, cin, ain, rin, total, sib, s_full, dinv, pot_all,
    load_sem, send_sem, recv_sem,
):
    blk = (blk0, blk1, blk2, blk3)
    box, face = lax.axis_index("box"), lax.axis_index("face")
    x, c = face // 2, face % 2
    other = 1 - c
    core_peer = (box, x * 2 + other)
    right = (box, ((x + 1) % 4) * 2 + c)
    left = (box, ((x + 3) % 4) * 2 + c)
    sibling = (box + 1 - 2 * (box % 2), face)
    sent = []

    def go(src, dst, where):
        i = len(sent)
        copy = pltpu.make_async_remote_copy(
            src_ref=src, dst_ref=dst, send_sem=send_sem.at[i], recv_sem=recv_sem.at[i],
            device_id=where, device_id_type=MESH,
        )
        copy.start()
        sent.append(copy)
        return copy

    box_of = [(x + q) % 4 for q in range(4)]
    loads = {
        q: pltpu.make_async_copy(blocks.at[box_of[q]], blk[q], load_sem.at[q]) for q in range(4)
    }
    load_sk = pltpu.make_async_copy(sketch, sk, load_sem.at[4])
    loads[2].start()
    loads[1].start()
    loads[3].start()
    loads[0].start()
    load_sk.start()

    barrier = pltpu.get_barrier_semaphore()
    for peer in (core_peer, right, left, sibling):
        pl.semaphore_signal(barrier, inc=1, device_id=peer, device_id_type=MESH)

    def slot(q, k):
        r = shared[box_of[q], k] - 3 * face
        own = jnp.where(jnp.logical_and(r >= 0, r < 3), 1, 0)
        return own, jnp.clip(r, 0, 2)

    def take_s(q):
        @pl.loop(0, 4)
        def _(k):
            own, r = slot(q, k)
            for half, ref in ((other, give), (c, keep)):
                for t in range(2):
                    j = shared[box_of[q], 2 * half + t]
                    w = own * pattern[r, box_of[q], j]
                    ref[t, q, pl.ds(k * B, B), :] = blk[q][r * 24 + j] * splat(w)

    def sketch_rows(q):
        b = box_of[q]

        inner = [shared[b, k] for k in range(4)]
        for j in range(24):
            ext = jnp.int32(1)
            for k in range(4):
                ext = ext * jnp.where(inner[k] == j, 0, 1)
            for r in range(3):
                w = splat(ext * pattern[r, b, j])
                am[r * B:(r + 1) * B, j * B:(j + 1) * B] = blk[q][r * 24 + j] * w

        acc = jnp.dot(am[...], sk[...], preferred_element_type=F32).astype(B16)
        for r in range(3):
            for h in range(2):
                yb[q, h, r] = acc[r * B:(r + 1) * B, h * B:(h + 1) * B]

        @pl.loop(0, 4)
        def _(k):
            own, r = slot(q, k)
            w = splat(own)
            give[2, q, pl.ds(k * B, B), :] = yb[q, other, r] * w
            keep[2, q, pl.ds(k * B, B), :] = yb[q, c, r] * w

    def take_side(q):
        b = box_of[q]

        @pl.loop(0, 3)
        def _(r):
            for l in range(4):
                j = shared[b, l]
                side[q, pl.ds(r * B, B), l * B:(l + 1) * B] = blk[q][r * 24 + j] * splat(pattern[r, b, j])

    swaps = {}

    def swap(t, q):
        swaps[t, q] = go(give.at[t, q], cin.at[t, q], core_peer)

    def merge(t, q):
        swaps[t, q].wait_recv()
        keep[t, q] = keep[t, q] + cin[t, q]

    jobs = [
        (0, (0, 256), (256, 256)),
        (1, (0, 256), (256, 256)),
        (2, (0, 128), (256, 128)),
        (2, (128, 128), (384, 128)),
    ]
    hops = {}

    def hop_a(n):
        t, h0, h1 = jobs[n]
        h0, h1 = pl.ds(*h0), pl.ds(*h1)
        hops["ar", n] = go(keep.at[t, 2, h0], ain.at[t, h0], right)
        hops["al", n] = go(keep.at[t, 2, h1], ain.at[t, h1], left)

    def hop_b(n):
        t, h0, h1 = jobs[n]
        h0, h1 = pl.ds(*h0), pl.ds(*h1)
        hops["br", n] = go(keep.at[t, 1, h1], rin.at[t, 0, h1], right)
        hops["bl", n] = go(keep.at[t, 3, h0], rin.at[t, 1, h0], left)

    def hop_c(n):
        t, h0, h1 = jobs[n]
        h0, h1 = pl.ds(*h0), pl.ds(*h1)
        hops["ar", n].wait_recv()
        keep[t, 1, h0] = keep[t, 1, h0] + ain[t, h0]
        hops["cr", n] = go(keep.at[t, 1, h0], rin.at[t, 0, h0], right)
        hops["al", n].wait_recv()
        keep[t, 3, h1] = keep[t, 3, h1] + ain[t, h1]
        hops["cl", n] = go(keep.at[t, 3, h1], rin.at[t, 1, h1], left)

    def to_sibling(n):
        t, h0, h1 = jobs[n]
        hops["s", n] = []
        for h, need in ((pl.ds(*h0), ("bl", "cr")), (pl.ds(*h1), ("br", "cl"))):
            for name in need:
                hops[name, n].wait_recv()
            total[t, h] = keep[t, 0, h] + rin[t, 0, h] + rin[t, 1, h]
            hops["s", n].append(go(total.at[t, h], sib.at[t, h], sibling))

    eye = lax.broadcasted_iota(jnp.int32, (B, B), 0) == lax.broadcasted_iota(jnp.int32, (B, B), 1)

    def sum_pair(t):
        for copy in hops["s", t]:
            copy.wait_recv()
        place = 2 * c + t
        s_full[place] = (total[t].astype(F32) + sib[t].astype(F32)).astype(B16)
        rows = pl.ds(pl.multiple_of(place * B, B), B)
        both = total[t, rows].astype(F32) + sib[t, rows].astype(F32)
        d = jnp.sum(jnp.where(eye, both, 0.0), axis=1, keepdims=True)
        dinv[place] = jnp.broadcast_to(1.0 / d, (B, B))
        s_full[place, rows] = jnp.where(eye, 0.0, both).astype(B16)
        return (
            go(s_full.at[place], s_full.at[place], core_peer),
            go(dinv.at[place], dinv.at[place], core_peer),
        )

    loads[2].wait()
    take_s(2)
    pl.semaphore_wait(barrier, 4)
    swap(0, 2)
    loads[1].wait()
    take_s(1)
    swap(0, 1)
    merge(0, 2)
    hop_a(0)
    loads[3].wait()
    take_s(3)
    swap(0, 3)
    swap(1, 2)
    merge(0, 1)
    merge(0, 3)
    hop_b(0)
    swap(1, 1)
    swap(1, 3)
    merge(1, 2)
    hop_a(1)
    merge(1, 1)
    merge(1, 3)
    loads[0].wait()
    take_s(0)
    swap(0, 0)
    swap(1, 0)
    load_sk.wait()
    sketch_rows(2)
    swap(2, 2)
    hop_c(0)
    hop_b(1)
    merge(0, 0)
    merge(1, 0)
    sketch_rows(1)
    swap(2, 1)
    hop_c(1)
    sketch_rows(3)
    swap(2, 3)
    merge(2, 2)
    hop_a(2)
    hop_a(3)
    to_sibling(0)
    merge(2, 1)
    merge(2, 3)
    hop_b(2)
    sketch_rows(0)
    swap(2, 0)
    to_sibling(1)
    hop_c(2)
    hop_b(3)
    merge(2, 0)
    for q in ORDER:
        take_side(q)
    halves = [*sum_pair(0)]
    hop_c(3)
    to_sibling(2)
    to_sibling(3)
    halves += sum_pair(1)
    for copy in hops["s", 2] + hops["s", 3] + halves:
        copy.wait_recv()

    early = len(sent) - 8
    for copy in sent[:early]:
        copy.wait_send()
    rhs = total[2].astype(F32) + sib[2].astype(F32)
    scale = dinv[...].reshape(4 * B, B)
    wide = jnp.concatenate([s_full[l] for l in range(4)], axis=1)
    pot = rhs * scale
    for _ in range(ITERS - 1):
        upper = pot.astype(B16)
        lower = (pot - upper.astype(F32)).astype(B16)
        terms = jnp.dot(wide, jnp.concatenate([upper, lower], axis=1), preferred_element_type=F32)
        pot = (rhs - (terms[:, :B] + terms[:, B:])) * scale
    pot_all[0, c] = pot.astype(B16)

    def correct(q, h):
        corr = jnp.dot(side[q], pot_all[q, h], preferred_element_type=F32)
        cols = pl.ds(pl.multiple_of(h * B, B), B)
        for r in range(3):
            rows = slice(r * B, (r + 1) * B)
            out[box_of[q], rows, cols] = (yb[q, h, r].astype(F32) - corr[rows]).astype(B16)

    top, low = pl.ds(0, 256), pl.ds(256, 256)

    def pass_on(q, h, where, to):
        return go(pot_all.at[q, c, h], pot_all.at[to, c, h], where)

    p3t = pass_on(0, top, right, 3)
    p1l = pass_on(0, low, left, 1)
    p3l = pass_on(0, low, right, 3)
    p1t = pass_on(0, top, left, 1)
    own = go(pot_all.at[0, c], pot_all.at[0, c], core_peer)
    correct(0, c)
    own.wait_recv()
    correct(0, other)
    p3t.wait_recv()
    f2t = pass_on(3, top, right, 2)
    p1l.wait_recv()
    f2l = pass_on(1, low, left, 2)
    p3l.wait_recv()
    e3 = go(pot_all.at[3, c], pot_all.at[3, c], core_peer)
    p1t.wait_recv()
    e1 = go(pot_all.at[1, c], pot_all.at[1, c], core_peer)
    correct(3, c)
    correct(1, c)
    f2t.wait_recv()
    e2t = pass_on(2, top, core_peer, 2)
    f2l.wait_recv()
    e2l = pass_on(2, low, core_peer, 2)
    e3.wait_recv()
    correct(3, other)
    e1.wait_recv()
    correct(1, other)
    correct(2, c)
    e2t.wait_recv()
    e2l.wait_recv()
    correct(2, other)
    for copy in sent[early:]:
        copy.wait_send()


N_COPIES = 64


def local(blocks, pattern, shared, sketch):
    boxes, rows, cols, blk, _ = blocks.shape
    order, width = sketch.shape
    blocks = blocks.reshape(boxes, rows * cols, blk, blk)
    pattern = pattern.transpose(1, 0, 2)
    v = pltpu.VMEM
    return pl.pallas_call(
        kernel,
        out_shape=v((boxes, rows * blk, width), B16),
        in_specs=[
            pl.BlockSpec(memory_space=pltpu.HBM),
            pl.BlockSpec(memory_space=pltpu.SMEM),
            pl.BlockSpec(memory_space=pltpu.SMEM),
            pl.BlockSpec(memory_space=pltpu.HBM),
        ],
        out_specs=pl.BlockSpec(memory_space=pltpu.VMEM),
        scratch_shapes=[
            *[v((rows * cols, blk, blk), B16) for _ in range(4)],
            v((order, width), B16),
            v((rows * blk, order), B16),
            v((4, 2, rows, blk, blk), B16),
            v((4, rows * blk, 512), B16),
            v((3, 4, 512, 128), B16), v((3, 4, 512, 128), B16), v((3, 4, 512, 128), B16),
            v((3, 512, 128), B16), v((3, 2, 512, 128), B16), v((3, 512, 128), B16), v((3, 512, 128), B16),
            v((4, 512, 128), B16), v((4, 128, 128), F32), v((4, 2, 512, 128), B16),
            pltpu.SemaphoreType.DMA((5,)),
            pltpu.SemaphoreType.DMA((N_COPIES,)),
            pltpu.SemaphoreType.DMA((N_COPIES,)),
        ],
        compiler_params=pltpu.CompilerParams(
            collective_id=0, has_side_effects=True, vmem_limit_bytes=56_000_000
        ),
        cost_estimate=pl.CostEstimate(flops=3_300_000_000, bytes_accessed=12_000_000, transcendentals=0),
    )(blocks, pattern, shared, sketch)


def solution(mesh):
    return jax.shard_map(
        local,
        mesh=mesh,
        in_specs=(P("box", "face", None, None, None), P("box", "face", None), P("box", None), P()),
        out_specs=P("box", "face", None),
        check_vma=False,
    )
```
